32 devices in a mesh: mp: 2 (over x), tok: 16 (over z, y, core).
Axes of the slice: x: 2, y: 2, z: 4, core: 2. Of those that a mesh axis runs over, the one named last changes fastest.
Arguments:
- inputs: bfloat16 [2, 16, 128, 2048], P('mp', 'tok'), may hold values from -6 to 6
- cotangent: bfloat16 [2, 16, 128, 4096], P('mp', 'tok'), may hold values from -6 to 6
- token_ids: int32 [2, 16, 128], P('mp', 'tok'), may hold values from 0 to 151935
- weights: float32 [2, 16, 256, 2048], P('mp', 'tok'), may hold values from -6 to 6
Outputs:
- merged: float32 [16, 256, 2048], P('tok')
The draws below stay inside these ranges and needn't reach their ends.
All inputs are finite; a program needn't handle non-finite values.
Results may differ from the reference program's by a relative error of at most 0.0003.
Values may be sent and summed in bfloat16 or wider, within the bound.
No kernel may reach another device: no remote copies, remote signals or barrier semaphores. Data moves between devices by JAX's collectives and lax.ppermute only.
A program may use at most 64 MiB of HBM per device.

```python
import math
import jax
import jax.numpy as jnp
from jax import lax

D = 2048
Q = 4096
VOCAB = 151936
TOK_SEQ = 128
ROW_BLOCKS = 8
FIRST_TEXT = 37984
MODELS = 2
SEQS = 16
BLOCKS = 16
COL_BLOCKS = 2
ROW_SPAN = 256
COL_SPAN = 2048


def touch_ends(values, own_key, least, largest):
    dims = values.shape
    spot = [jax.random.randint(jax.random.fold_in(own_key, axis), (), 0, dims[axis]) for axis in range(len(dims))]
    values = values.at[tuple(spot)].set(least)
    longest = dims.index(max(dims))
    spot[longest] = (spot[longest] + 1) % dims[longest]
    return values.at[tuple(spot)].set(largest)


def levels(key, shape, shards, least, high):
    level, own = 1.0, jax.random.fold_in(key, 6)
    for axis_at, shards_of in shards:
        heights = jnp.exp(jax.random.uniform(jax.random.fold_in(own, axis_at), (shards_of,), jnp.float32, least / len(shards), high / len(shards)))
        level = level * jnp.repeat(heights, shape[axis_at] // shards_of).reshape([-1 if axis == axis_at else 1 for axis in range(len(shape))])
    return level


def centred(own_key, shape, scale, bound, shards=(), held_as=jnp.bfloat16):
    result = scale * jax.random.normal(own_key, shape, jnp.float32)
    if shards:
        result = result * levels(own_key, shape, shards, -0.22, 0.18)
    return jnp.clip(result, -bound, bound).astype(held_as)


def setup_inputs(seed: int = 0) -> dict:
    keys = jax.random.split(jax.random.key(seed), 5)
    return {
        "inputs": centred(keys[0], (MODELS, SEQS, TOK_SEQ, D), 1.0, 6.0, ((0, 2), (1, 16))),
        "cotangent": centred(keys[1], (MODELS, SEQS, TOK_SEQ, Q), 1.0, 6.0, ((0, 2), (1, 16))),
        "token_ids": touch_ends(jax.random.randint(keys[2], (MODELS, SEQS, TOK_SEQ), 0, VOCAB), jax.random.fold_in(keys[2], 1), 0, VOCAB - 1).astype(jnp.int32),
        "weights": centred(keys[3], (MODELS, BLOCKS, ROW_SPAN, COL_SPAN), 1.0, 6.0, ((0, 2), (1, 16)), jnp.float32),
    }


damping = 0.1

def one_model(bundle):
    activations, cotangents, identifiers = bundle

    def accumulate(summed, sequence):
        act_rows, cot_rows, id_rows = sequence
        kept_mask = (id_rows >= FIRST_TEXT).astype(jnp.bfloat16)
        masked = cot_rows * kept_mask[:, None]
        gradient = jnp.dot(act_rows.T, masked, preferred_element_type=jnp.float32) / math.sqrt(TOK_SEQ)
        return (summed + gradient * gradient, None)
    start = jnp.zeros((D, Q), jnp.float32)
    summed, unused = lax.scan(accumulate, start, (activations, cotangents, identifiers))
    fisher = summed / SEQS
    blocked = fisher.reshape(ROW_BLOCKS, ROW_SPAN, COL_BLOCKS, COL_SPAN).transpose(0, 2, 1, 3)
    return blocked.reshape(BLOCKS, ROW_SPAN, COL_SPAN) + damping

def reference(inputs, cotangent, token_ids, weights):
    damped = lax.map(one_model, (inputs, cotangent, token_ids))
    return lax.optimization_barrier(jnp.sum(damped * weights, axis=0)) / lax.optimization_barrier(jnp.sum(damped, axis=0))
```

```python
import functools
import math

import jax
import jax.numpy as jnp
from jax import lax
from jax.experimental import pallas as pl
from jax.experimental.pallas import tpu as pltpu
from jax.sharding import Mesh
from jax.sharding import PartitionSpec as P

ROW_BLOCKS = 8
FIRST_TEXT = 37984
LARGEST = 6.0

damping = 0.1

TOK = ("zh", "zl", "y", "c")
VMEM = pl.BlockSpec(memory_space=pltpu.VMEM)
VMEM_LIMIT = 48 * 1024 * 1024
CHUNKS = (0.5, 0.5)


def swap(value, axes):
    if isinstance(axes, str):
        return lax.ppermute(value, axes, [(0, 1), (1, 0)])
    return lax.ppermute(value, axes, [(i, i ^ 3) for i in range(4)])


def rotate(value, axis, offset):
    size = lax.axis_size(axis)
    return lax.ppermute(value, axis, [(i, (i + offset) % size) for i in range(size)])


def call(body, out_shape, scratch_shapes=(), flops=0, bytes_accessed=0):
    def run(*args):
        return pl.pallas_call(
            body,
            out_shape=out_shape,
            in_specs=[VMEM] * len(args),
            out_specs=jax.tree.map(lambda _: VMEM, out_shape),
            scratch_shapes=list(scratch_shapes),
            compiler_params=pltpu.CompilerParams(vmem_limit_bytes=VMEM_LIMIT),
            cost_estimate=pl.CostEstimate(flops=flops, bytes_accessed=bytes_accessed, transcendentals=0),
        )(*args)

    return run


def row_kernel(inputs_ref, keep_ref, send_ref):
    half = keep_ref.shape[1]
    own = lax.axis_index("zh")
    for ref, part in ((keep_ref, own), (send_ref, 1 - own)):
        for s in range(inputs_ref.shape[0]):
            start = pl.multiple_of(part * half, half)
            ref[s] = inputs_ref[s, :, pl.ds(start, half)].T


def col_kernel(ids_ref, cot_ref, *outs):
    seqs, length, width = ids_ref.shape[0], cot_ref.shape[1], outs[0].shape[3]
    core_count = len(outs) // 2
    own_y, own_c = lax.axis_index("y"), lax.axis_index("c")
    for s in range(seqs):
        kept = jnp.broadcast_to((ids_ref[s : s + 1, :] >= FIRST_TEXT).astype(jnp.float32), (128, length)).T
        kept = kept[:, :1] > 0.5
        for at, ref in enumerate(outs):
            to_y = own_y ^ (at // core_count)
            to_c = lax.rem(own_c + at % core_count, core_count)
            for zl in range(2):
                start = pl.multiple_of(((to_c * 2 + zl) * 2 + to_y) * width, width)
                piece = cot_ref[s, :, pl.ds(start, width)]
                ref[zl, s] = jnp.where(kept, piece, jnp.zeros_like(piece))


def pack_kernel(widths, *refs):
    count = len(refs) - 2 * len(widths)
    ins, outs = refs[:count], refs[count:]
    own = lax.axis_index("zl")
    start = 0
    for at, width in enumerate(widths):
        for which in range(2):
            ref = outs[2 * at + which]
            for i, source in enumerate(ins):
                seqs = source.shape[1]
                ref[i * seqs : (i + 1) * seqs] = source[own ^ which, :, :, start : start + width]
        start += width


def fisher_kernel(row_count, scale, code_scale, *refs):
    rows, cols, outs, total = refs[:row_count], refs[row_count:-5], refs[-5:-1], refs[-1]
    span = outs[0].shape[0]
    own_zl, own_y = lax.axis_index("zl"), lax.axis_index("y")
    per = row_count // len(cols)

    seqs = rows[0].shape[0]
    for group in range(4):
        part = slice(group * span, (group + 1) * span)
        acc = None
        for r in range(row_count):
            for s in range(seqs):
                g = jnp.dot(
                    rows[r][s, part, :], cols[r // per][(r % per) * seqs + s], preferred_element_type=jnp.float32
                )
                acc = g * g if acc is None else acc + g * g
        damped = acc * scale + damping
        code = jnp.round((jnp.log(damped) - math.log(damping)) * code_scale) - 32768.0
        total[part, :] = jnp.clip(code, -32768.0, 32767.0)
    for at, ref in enumerate(outs):
        group = (own_zl ^ (at // 2)) * 2 + (own_y ^ (at % 2))
        start = pl.multiple_of(group * span, span)
        ref[...] = total[pl.ds(start, span), :].astype(jnp.int32).astype(jnp.int16)


def merge_kernel(models, widths, code_scale, *refs):
    weights, codes, out = refs[:models], refs[models:-1], refs[-1]
    chunk_count = len(widths)
    own_zl, own_y, own_m = lax.axis_index("zl"), lax.axis_index("y"), lax.axis_index("mp")

    def pick(values, j):
        chosen = values[0]
        for offset in range(1, models):
            chosen = jnp.where(lax.rem(own_m + models - offset, models) == j, values[offset], chosen)
        return chosen

    for at in range(4):
        sub = (own_zl ^ (at // 2)) * 2 + (own_y ^ (at % 2))
        first = 0
        for k, width in enumerate(widths):
            start = pl.multiple_of(sub * sum(widths) + first, 128)
            first += width
            damped, weight = [], []
            for m in range(models):
                code = codes[(m * 4 + at) * chunk_count + k][...].astype(jnp.int32).astype(jnp.float32)
                damped.append(jnp.exp((code + 32768.0) * (1.0 / code_scale) + math.log(damping)))
                weight.append(weights[m][:, pl.ds(start, width)])
            num, den = None, None
            for j in range(models):
                d = pick(damped, j)
                p = d * pick(weight, j)
                num = p if num is None else num + p
                den = d if den is None else den + d
            out[:, pl.ds(start, width)] = num / den


def shards(inputs, cotangent, token_ids, weights):
    models = lax.axis_size("mp")
    core_count = lax.axis_size("c")
    inputs, cotangent, token_ids, weights = inputs[0], cotangent[0], token_ids[0], weights[0, 0]
    seqs, length, feature_width = inputs.shape
    query_width = cotangent.shape[2]
    bf = jnp.bfloat16
    half = feature_width // 2
    tile_width = query_width // (4 * core_count)
    span = half // 4
    total_seqs = seqs * 8 * core_count
    widths = [int(tile_width * part) for part in CHUNKS]
    if any(width % 128 for width in widths):
        widths = [tile_width]
    peak = LARGEST**4 * length + damping
    code_scale = 65535.0 / (math.log(peak) - math.log(damping))

    other_weights = [rotate(weights, "mp", offset) for offset in range(1, models)]

    row_shape = jax.ShapeDtypeStruct((seqs, half, length), bf)
    keep, send = pl.pallas_call(
        row_kernel,
        out_shape=(row_shape, row_shape),
        in_specs=[VMEM],
        out_specs=(VMEM, VMEM),
        compiler_params=pltpu.CompilerParams(vmem_limit_bytes=VMEM_LIMIT),
    )(inputs)
    col_shape = jax.ShapeDtypeStruct((2, seqs, length, tile_width), bf)
    col_parts = call(col_kernel, (col_shape,) * (2 * core_count))(token_ids, cotangent)

    z2 = swap(send, "zh")
    z1 = swap(keep, "zl")
    z3 = swap(z2, "zl")
    by_z = [keep, z1, z2, z3]
    by_zy = [[r, swap(r, "y")] for r in by_z]
    rows = [[[r] + [rotate(r, "c", o) for o in range(1, core_count)] for r in pair] for pair in by_zy]
    rows = [r for a in rows for b in a for r in b]

    got = []
    for at, part in enumerate(col_parts):
        dy, dc = at // core_count, at % core_count
        if dy and dc:
            size = 2 * core_count
            perm = []
            for i in range(size):
                y, c = i // core_count, i % core_count
                perm.append((i, (y ^ 1) * core_count + (c + dc) % core_count))
            part = lax.ppermute(part, ("y", "c"), perm)
        elif dy:
            part = swap(part, "y")
        elif dc:
            part = rotate(part, "c", dc)
        got.append(part)
    pack_shapes = []
    for width in widths:
        pack_shapes += [jax.ShapeDtypeStruct((seqs * 2 * core_count, length, width), bf)] * 2
    packed = call(functools.partial(pack_kernel, widths), tuple(pack_shapes))(*got)

    codes = []
    for k, width in enumerate(widths):
        own, other = packed[2 * k], packed[2 * k + 1]
        cols = [own, swap(other, "zl"), swap(own, "zh"), swap(other, ("zh", "zl"))]
        code_shape = jax.ShapeDtypeStruct((span, width), jnp.int16)
        outs = call(
            functools.partial(fisher_kernel, len(rows), 1.0 / (length * total_seqs), code_scale),
            (code_shape,) * 4,
            [pltpu.VMEM((half, width), jnp.float32)],
            flops=2 * half * width * length * total_seqs,
            bytes_accessed=2 * length * total_seqs * (half + width),
        )(*rows, *cols)
        codes.append([outs[0], swap(outs[1], "y"), swap(outs[2], "zl"), swap(outs[3], ("zl", "y"))])

    own_codes = [codes[k][at] for at in range(4) for k in range(len(widths))]
    all_codes = list(own_codes)
    for offset in range(1, models):
        all_codes += [rotate(code, "mp", offset) for code in own_codes]
    merged = call(
        functools.partial(merge_kernel, models, widths, code_scale),
        jax.ShapeDtypeStruct(weights.shape, jnp.float32),
    )(weights, *other_weights, *all_codes)
    return merged[None]


def solution(mesh):
    models, devices = mesh.shape["mp"], mesh.shape["tok"]
    grid = Mesh(mesh.devices.reshape(models, 2, 2, ROW_BLOCKS // 4, devices // ROW_BLOCKS), ("mp",) + TOK)
    in_specs = (
        P("mp", TOK, None, None),
        P("mp", TOK, None, None),
        P("mp", TOK, None),
        P("mp", TOK, None, None),
    )
    return jax.shard_map(shards, mesh=grid, in_specs=in_specs, out_specs=P(TOK, None, None), check_vma=False)
```

```python
import functools
import math

import jax
import jax.numpy as jnp
from jax import lax
from jax.experimental import pallas as pl
from jax.experimental.pallas import tpu as pltpu
from jax.sharding import Mesh
from jax.sharding import PartitionSpec as P

ROW_BLOCKS = 8
FIRST_TEXT = 37984
LARGEST = 6.0

damping = 0.1

TOK = ("zh", "zl", "y", "c")
VMEM = pl.BlockSpec(memory_space=pltpu.VMEM)
VMEM_LIMIT = 48 * 1024 * 1024

CHUNKS = (0.5, 0.5)


def swap(value, axes):
    if isinstance(axes, str):
        return lax.ppermute(value, axes, [(0, 1), (1, 0)])
    return lax.ppermute(value, axes, [(i, i ^ 3) for i in range(4)])


def rotate(value, axis, offset):
    size = lax.axis_size(axis)
    return lax.ppermute(value, axis, [(i, (i + offset) % size) for i in range(size)])


def call(body, out_shape, scratch_shapes=(), flops=0, bytes_accessed=0):
    def run(*args, after=()):
        def kernel(*refs):
            body(*refs[: len(args)], *refs[len(args) + len(after) :])

        return pl.pallas_call(
            kernel,
            out_shape=out_shape,
            in_specs=[VMEM] * len(args) + [pl.BlockSpec(memory_space=pl.ANY)] * len(after),
            out_specs=jax.tree.map(lambda _: VMEM, out_shape),
            scratch_shapes=list(scratch_shapes),
            compiler_params=pltpu.CompilerParams(vmem_limit_bytes=VMEM_LIMIT),
            cost_estimate=pl.CostEstimate(flops=flops, bytes_accessed=bytes_accessed, transcendentals=0),
        )(*args, *after)

    return run


def front_kernel(inputs_ref, ids_ref, cot_ref, keep_ref, send_ref, *outs):
    half = keep_ref.shape[1]
    own = lax.axis_index("zh")
    for ref, part in ((keep_ref, own), (send_ref, 1 - own)):
        for s in range(inputs_ref.shape[0]):
            start = pl.multiple_of(part * half, half)
            ref[s] = inputs_ref[s, :, pl.ds(start, half)].T
    seqs, length, width = ids_ref.shape[0], cot_ref.shape[1], outs[0].shape[3]
    core_count = len(outs) // 2
    own_y, own_c = lax.axis_index("y"), lax.axis_index("c")
    for s in range(seqs):
        kept = jnp.broadcast_to((ids_ref[s : s + 1, :] >= FIRST_TEXT).astype(jnp.float32), (128, length)).T
        kept = kept[:, :1] > 0.5
        for at, ref in enumerate(outs):
            to_y = own_y ^ (at // core_count)
            to_c = lax.rem(own_c + at % core_count, core_count)
            for zl in range(2):
                start = pl.multiple_of(((to_c * 2 + zl) * 2 + to_y) * width, width)
                piece = cot_ref[s, :, pl.ds(start, width)]
                ref[zl, s] = jnp.where(kept, piece, jnp.zeros_like(piece))


def fill(out, *refs):
    at = 0
    for ref in refs:
        out[at : at + ref.shape[0]] = ref[...]
        at += ref.shape[0]


def pack(start, own_ref, other_ref, sources):
    own, width = lax.axis_index("zl"), own_ref.shape[2]
    for which, ref in enumerate((own_ref, other_ref)):
        for i, source in enumerate(sources):
            seqs = source.shape[1]
            ref[i * seqs : (i + 1) * seqs] = source[own ^ which, :, :, start : start + width]


def gather_kernel(keep, z1, z2, *refs):
    near, joint, own_ref, other_ref = refs[-4:]
    fill(near, keep, z1, z2)
    pack(0, own_ref, other_ref, refs[:-4])
    at = 0
    for s in range(z2.shape[0]):
        joint[at : at + z2.shape[1], :] = z2[s]
        at += z2.shape[1]
    count, length, width = other_ref.shape
    for i in range(count):
        for start in range(0, width, 128):
            joint[at : at + length, :] = other_ref[i, :, start : start + 128]
            at += length


def second_kernel(starts, near, joint, *refs):
    count = 3 + 2 * len(starts)
    sources, (own_rows, far, cols, *outs) = refs[:-count], refs[-count:]
    at = 0
    for s in range(far.shape[0]):
        far[s] = joint[at : at + far.shape[1], :]
        at += far.shape[1]
    fill(own_rows, near, far)
    count, length, width = cols.shape
    for i in range(count):
        for start in range(0, width, 128):
            cols[i, :, start : start + 128] = joint[at : at + length, :]
            at += length
    for k, start in enumerate(starts):
        pack(start, outs[2 * k], outs[2 * k + 1], sources)


def third_kernel(first, second, out):
    fill(out, first, second)


def code_kernel(*refs):
    for at, ref in enumerate(refs[:-1]):
        refs[-1][at] = ref[...]


def fisher_kernel(places, row_count, scale, code_scale, *refs):
    rows, cols, outs, total = refs[:row_count], refs[row_count:-5], refs[-5:-1], refs[-1]
    span = outs[0].shape[0]
    own_zl, own_y = lax.axis_index("zl"), lax.axis_index("y")

    for group in range(4):
        part = slice(group * span, (group + 1) * span)
        acc = None
        for row_at, row_sub, col_at, col_sub in places:
            g = jnp.dot(rows[row_at][row_sub, part, :], cols[col_at][col_sub], preferred_element_type=jnp.float32)
            acc = g * g if acc is None else acc + g * g
        damped = acc * scale + damping
        code = jnp.round((jnp.log(damped) - math.log(damping)) * code_scale) - 32768.0
        total[part, :] = jnp.clip(code, -32768.0, 32767.0)
    for at, ref in enumerate(outs):
        group = (own_zl ^ (at // 2)) * 2 + (own_y ^ (at % 2))
        start = pl.multiple_of(group * span, span)
        ref[...] = total[pl.ds(start, span), :].astype(jnp.int32).astype(jnp.int16)


def merge_chunk(models, tile_width, first, width, code_scale, weights, codes, store):
    own_zl, own_y, own_m = lax.axis_index("zl"), lax.axis_index("y"), lax.axis_index("mp")

    def pick(values, j):
        chosen = values[0]
        for offset in range(1, models):
            chosen = jnp.where(lax.rem(own_m + models - offset, models) == j, values[offset], chosen)
        return chosen

    for at in range(4):
        sub = (own_zl ^ (at // 2)) * 2 + (own_y ^ (at % 2))
        start = pl.multiple_of(sub * tile_width + first, 128)
        codes_here = [code[at].astype(jnp.int32) for code in codes]
        weights_here = [weight[:, pl.ds(start, width)] for weight in weights]
        base = pick(codes_here, 0)
        num, den = pick(weights_here, 0), None
        for j in range(1, models):
            ratio = jnp.exp((pick(codes_here, j) - base).astype(jnp.float32) * (1.0 / code_scale))
            num = num + ratio * pick(weights_here, j)
            den = 1.0 + ratio if den is None else den + ratio
        store(at, start, num if den is None else num / den)


def early_merge_kernel(models, tile_width, first, width, code_scale, *refs):
    def store(at, start, value):
        refs[-1][at] = value

    weights, codes = refs[:models], refs[models:-1]
    merge_chunk(models, tile_width, first, width, code_scale, weights, codes, store)


def last_merge_kernel(models, tile_width, firsts, width, code_scale, *refs):
    weights, codes, early, out = refs[:models], refs[models : 2 * models], refs[2 * models : -1], refs[-1]
    own_zl, own_y = lax.axis_index("zl"), lax.axis_index("y")
    for first, ref in zip(firsts, early):
        for at in range(4):
            sub = (own_zl ^ (at // 2)) * 2 + (own_y ^ (at % 2))
            start = pl.multiple_of(sub * tile_width + first, 128)
            out[:, pl.ds(start, ref.shape[2])] = ref[at]

    def store(at, start, value):
        out[:, pl.ds(start, width)] = value

    merge_chunk(models, tile_width, firsts[-1], width, code_scale, weights, codes, store)


def shards(inputs, cotangent, token_ids, weights):
    models = lax.axis_size("mp")
    core_count = lax.axis_size("c")
    inputs, cotangent, token_ids, weights = inputs[0], cotangent[0], token_ids[0], weights[0, 0]
    seqs, length, feature_width = inputs.shape
    query_width = cotangent.shape[2]
    bf = jnp.bfloat16
    half = feature_width // 2
    tile_width = query_width // (4 * core_count)
    span = half // 4
    total_seqs = seqs * 8 * core_count
    widths = [int(tile_width * part) for part in CHUNKS]
    if any(width % 128 for width in widths):
        widths = [tile_width]
    peak = LARGEST**4 * length + damping
    code_scale = 65535.0 / (math.log(peak) - math.log(damping))

    other_weights = [rotate(weights, "mp", offset) for offset in range(1, models)]

    col_shape = jax.ShapeDtypeStruct((2, seqs, length, tile_width), bf)
    row_shape = jax.ShapeDtypeStruct((seqs, half, length), bf)
    keep, send, *col_parts = call(front_kernel, (row_shape,) * 2 + (col_shape,) * (2 * core_count))(
        inputs, token_ids, cotangent
    )

    got = []
    for at, part in enumerate(col_parts):
        dy, dc = at // core_count, at % core_count
        if dy and dc:
            size = 2 * core_count
            perm = []
            for i in range(size):
                y, c = i // core_count, i % core_count
                perm.append((i, (y ^ 1) * core_count + (c + dc) % core_count))
            part = lax.ppermute(part, ("y", "c"), perm)
        elif dy:
            part = swap(part, "y")
        elif dc:
            part = rotate(part, "c", dc)
        got.append(part)

    starts = [sum(widths[:k]) for k in range(len(widths))]

    def several(count, width):
        return jax.ShapeDtypeStruct((seqs * count, length, width), bf)

    def many_rows(count):
        return jax.ShapeDtypeStruct((seqs * count, half, length), bf)

    z2 = swap(send, "zh")
    z1 = swap(keep, "zl")
    packs = [None] * len(widths)
    pieces = seqs * (half + 2 * core_count * length * (widths[0] // 128))
    near, joint, own, other = call(
        gather_kernel,
        (many_rows(3), jax.ShapeDtypeStruct((pieces, length), bf)) + (several(2 * core_count, widths[0]),) * 2,
    )(keep, z1, z2, *got)
    packs[0] = [own, other]
    pack_shapes = [several(2 * core_count, width) for width in widths[1:] for _ in range(2)]
    own_rows, far, near_cols, *others = call(
        functools.partial(second_kernel, starts[1:]),
        (many_rows(4), many_rows(1), several(2 * core_count, widths[0])) + tuple(pack_shapes),
    )(near, swap(joint, "zl"), *got)
    for k in range(1, len(widths)):
        packs[k] = others[2 * k - 2 : 2 * k]
    first_cols = [packs[0][0], near_cols, swap(packs[0][0], "zh"), swap(packs[0][1], ("zh", "zl"))]
    y_rows = call(third_kernel, many_rows(4))(swap(near, "y"), swap(far, "y"), after=first_cols[2:])
    rows = []
    for dc in range(core_count):
        rows += [own_rows, y_rows] if dc == 0 else [rotate(own_rows, "c", dc), rotate(y_rows, "c", dc)]
    places = []
    for dz in range(4):
        for dy in range(2):
            for dc in range(core_count):
                for s in range(seqs):
                    places.append((dc * 2 + dy, dz * seqs + s, dz, (dy * core_count + dc) * seqs + s))

    merged = []
    for k, width in enumerate(widths):
        own, other = packs[k]
        cols = [own, swap(other, "zl"), swap(own, "zh"), swap(other, ("zh", "zl"))] if k else first_cols
        code_shape = jax.ShapeDtypeStruct((span, width), jnp.int16)
        outs = call(
            functools.partial(fisher_kernel, places, len(rows), 1.0 / (length * total_seqs), code_scale),
            (code_shape,) * 4,
            [pltpu.VMEM((half, width), jnp.float32)],
            flops=2 * half * width * length * total_seqs,
            bytes_accessed=2 * length * total_seqs * (half + width),
        )(*rows, *cols)
        codes = call(code_kernel, jax.ShapeDtypeStruct((4, span, width), jnp.int16))(
            outs[0],
            swap(outs[1], "y"),
            swap(outs[2], "zl"),
            swap(outs[3], ("zl", "y")),
            after=() if k else other_weights,
        )
        all_codes = [codes] + [rotate(codes, "mp", offset) for offset in range(1, models)]
        if k < len(widths) - 1:
            merged.append(
                call(
                    functools.partial(early_merge_kernel, models, tile_width, starts[k], width, code_scale),
                    jax.ShapeDtypeStruct((4, span, width), jnp.float32),
                )(weights, *other_weights, *all_codes)
            )
        else:
            result = call(
                functools.partial(last_merge_kernel, models, tile_width, starts, width, code_scale),
                jax.ShapeDtypeStruct(weights.shape, jnp.float32),
            )(weights, *other_weights, *all_codes, *merged)
    return result[None]


def solution(mesh):
    models, devices = mesh.shape["mp"], mesh.shape["tok"]
    grid = Mesh(mesh.devices.reshape(models, 2, 2, ROW_BLOCKS // 4, devices // ROW_BLOCKS), ("mp",) + TOK)
    in_specs = (
        P("mp", TOK, None, None),
        P("mp", TOK, None, None),
        P("mp", TOK, None),
        P("mp", TOK, None, None),
    )
    return jax.shard_map(shards, mesh=grid, in_specs=in_specs, out_specs=P(TOK, None, None), check_vma=False)
```

```python
import functools
import math

import jax
import jax.numpy as jnp
from jax import lax
from jax.experimental import pallas as pl
from jax.experimental.pallas import tpu as pltpu
from jax.sharding import Mesh
from jax.sharding import PartitionSpec as P

ROW_BLOCKS = 8
FIRST_TEXT = 37984
LARGEST = 6.0

damping = 0.1

TOK = ("zh", "zl", "y", "c")
VMEM = pl.BlockSpec(memory_space=pltpu.VMEM)
VMEM_LIMIT = 48 * 1024 * 1024

CHUNKS = (0.5, 0.5)


def swap(value, axes):
    if isinstance(axes, str):
        return lax.ppermute(value, axes, [(0, 1), (1, 0)])
    return lax.ppermute(value, axes, [(i, i ^ 3) for i in range(4)])


def rotate(value, axis, offset):
    size = lax.axis_size(axis)
    return lax.ppermute(value, axis, [(i, (i + offset) % size) for i in range(size)])


def call(body, out_shape, scratch_shapes=(), flops=0, bytes_accessed=0):
    def run(*args, after=()):
        def kernel(*refs):
            body(*refs[: len(args)], *refs[len(args) + len(after) :])

        return pl.pallas_call(
            kernel,
            out_shape=out_shape,
            in_specs=[VMEM] * len(args) + [pl.BlockSpec(memory_space=pl.ANY)] * len(after),
            out_specs=jax.tree.map(lambda _: VMEM, out_shape),
            scratch_shapes=list(scratch_shapes),
            compiler_params=pltpu.CompilerParams(vmem_limit_bytes=VMEM_LIMIT),
            cost_estimate=pl.CostEstimate(flops=flops, bytes_accessed=bytes_accessed, transcendentals=0),
        )(*args, *after)

    return run


def front_kernel(inputs_ref, ids_ref, cot_ref, keep_ref, send_ref, *outs):
    half = keep_ref.shape[1]
    own = lax.axis_index("zh")
    for ref, part in ((keep_ref, own), (send_ref, 1 - own)):
        for s in range(inputs_ref.shape[0]):
            start = pl.multiple_of(part * half, half)
            ref[s] = inputs_ref[s, :, pl.ds(start, half)].T
    seqs, length, width = ids_ref.shape[0], cot_ref.shape[1], outs[0].shape[3]
    core_count = len(outs) // 2
    own_y, own_c = lax.axis_index("y"), lax.axis_index("c")
    for s in range(seqs):
        kept = jnp.broadcast_to((ids_ref[s : s + 1, :] >= FIRST_TEXT).astype(jnp.float32), (128, length)).T
        kept = kept[:, :1] > 0.5
        for at, ref in enumerate(outs):
            to_y = own_y ^ (at // core_count)
            to_c = lax.rem(own_c + at % core_count, core_count)
            for zl in range(2):
                start = pl.multiple_of(((to_c * 2 + zl) * 2 + to_y) * width, width)
                piece = cot_ref[s, :, pl.ds(start, width)]
                ref[zl, s] = jnp.where(kept, piece, jnp.zeros_like(piece))


def fill(out, *refs):
    at = 0
    for ref in refs:
        out[at : at + ref.shape[0]] = ref[...]
        at += ref.shape[0]


def pack(start, own_ref, other_ref, sources):
    own, width = lax.axis_index("zl"), other_ref.shape[2]
    for which, ref in enumerate((own_ref, other_ref)):
        for i, source in enumerate(sources):
            seqs = source.shape[1]
            ref[i * seqs : (i + 1) * seqs] = source[own ^ which, :, :, start : start + width]


def gather_kernel(keep, z1, z2, *refs):
    near, pass_on, own_ref, other_ref = refs[-4:]
    fill(near, keep, z1, z2)
    fill(pass_on, z2)
    pack(0, own_ref, other_ref, refs[:-4])


def second_kernel(starts, near, z3, *refs):
    count = 2 + 2 * len(starts)
    sources, (own_rows, far, *outs) = refs[:-count], refs[-count:]
    fill(far, z3)
    fill(own_rows, near, z3)
    for k, start in enumerate(starts):
        pack(start, outs[2 * k], outs[2 * k + 1], sources)


def third_kernel(own, first, second, out):
    fill(out, own, first, second)


def code_kernel(*refs):
    for at, ref in enumerate(refs[:-1]):
        refs[-1][at] = ref[...]


def fisher_kernel(places, row_count, scale, code_scale, *refs):
    rows, cols, outs, total = refs[:row_count], refs[row_count : row_count + 4], refs[row_count + 4 : -1], refs[-1]
    span = total.shape[0] // 4
    own_zl, own_y = lax.axis_index("zl"), lax.axis_index("y")

    for group in range(4):
        part = slice(group * span, (group + 1) * span)
        acc = None
        for row_at, row_sub, col_at, col_sub in places:
            g = jnp.dot(rows[row_at][row_sub, part, :], cols[col_at][col_sub], preferred_element_type=jnp.float32)
            acc = g * g if acc is None else acc + g * g
        damped = acc * scale + damping
        code = jnp.round((jnp.log(damped) - math.log(damping)) * code_scale) - 32768.0
        total[part, :] = jnp.clip(code, -32768.0, 32767.0)
    for at in range(4):
        group = (own_zl ^ (at // 2)) * 2 + (own_y ^ (at % 2))
        start = pl.multiple_of(group * span, span)
        code = total[pl.ds(start, span), :].astype(jnp.int32).astype(jnp.int16)
        if len(outs) == 1:
            outs[0][at] = code
        else:
            outs[at][...] = code


def models_kernel(models, *refs):
    for at, out in enumerate(refs[models:]):
        for m in range(models):
            out[m] = refs[m][at]


def merge_chunk(models, tile_width, first, width, code_scale, weights, codes, store):
    own_zl, own_y, own_m = lax.axis_index("zl"), lax.axis_index("y"), lax.axis_index("mp")

    def pick(values, j):
        chosen = values[0]
        for offset in range(1, models):
            chosen = jnp.where(lax.rem(own_m + models - offset, models) == j, values[offset], chosen)
        return chosen

    for at in range(4):
        sub = (own_zl ^ (at // 2)) * 2 + (own_y ^ (at % 2))
        start = pl.multiple_of(sub * tile_width + first, 128)
        codes_here = [codes(m, at).astype(jnp.int32) for m in range(models)]
        weights_here = [weights[0][:, pl.ds(start, width)]]
        for m in range(1, models):
            halves = [half[:, pl.ds(start, width)] for half in weights[2 * m - 1 : 2 * m + 1]]
            weights_here.append(jnp.concatenate(halves, axis=0))
        base = pick(codes_here, 0)
        num, den = pick(weights_here, 0), None
        for j in range(1, models):
            ratio = jnp.exp((pick(codes_here, j) - base).astype(jnp.float32) * (1.0 / code_scale))
            num = num + ratio * pick(weights_here, j)
            den = 1.0 + ratio if den is None else den + ratio
        store(at, start, num if den is None else num / den)


def early_merge_kernel(models, tile_width, first, width, code_scale, *refs):
    def store(at, start, value):
        refs[-1][at] = value

    weights, codes = refs[: 2 * models - 1], refs[2 * models - 1 : -1]
    merge_chunk(models, tile_width, first, width, code_scale, weights, lambda m, at: codes[m][at], store)


def last_merge_kernel(models, tile_width, firsts, widths, code_scale, *refs):
    early, out, parts, done = refs[0], refs[-3], refs[-2], refs[-1]
    weights, codes = refs[1 : 2 * models], refs[2 * models : -3]
    own_zl, own_y = lax.axis_index("zl"), lax.axis_index("y")
    copies = []

    def send(source, start, width):
        copies.append(pltpu.make_async_copy(source, out.at[:, pl.ds(start, width)], done.at[len(copies)]))
        copies[-1].start()

    for at in range(4):
        sub = (own_zl ^ (at // 2)) * 2 + (own_y ^ (at % 2))
        send(early.at[at], pl.multiple_of(sub * tile_width + firsts[-1], 128), widths[-1])
    for k, width in enumerate(widths[:-1]):

        def store(at, start, value):
            parts[at, :, firsts[k] : firsts[k] + width] = value
            send(parts.at[at, :, pl.ds(firsts[k], width)], start, width)

        here = codes[4 * k : 4 * k + 4]
        merge_chunk(models, tile_width, firsts[k], width, code_scale, weights, lambda m, at: here[at][m], store)
    for copy in copies:
        copy.wait()


def shards(inputs, cotangent, token_ids, weights):
    models = lax.axis_size("mp")
    core_count = lax.axis_size("c")
    inputs, cotangent, token_ids, weights = inputs[0], cotangent[0], token_ids[0], weights[0, 0]
    seqs, length, feature_width = inputs.shape
    query_width = cotangent.shape[2]
    bf = jnp.bfloat16
    half = feature_width // 2
    tile_width = query_width // (4 * core_count)
    span = half // 4
    total_seqs = seqs * 8 * core_count
    widths = [int(tile_width * part) for part in CHUNKS]
    if any(width % 128 for width in widths):
        widths = [tile_width]
    peak = LARGEST**4 * length + damping
    code_scale = 65535.0 / (math.log(peak) - math.log(damping))

    early_rows = weights.shape[0] // 2
    other_weights = []
    for offset in range(1, models):
        other_weights += [rotate(weights[:early_rows], "mp", offset), rotate(weights[early_rows:], "mp", offset)]

    col_shape = jax.ShapeDtypeStruct((2, seqs, length, tile_width), bf)
    row_shape = jax.ShapeDtypeStruct((seqs, half, length), bf)
    keep, send, *col_parts = call(front_kernel, (row_shape,) * 2 + (col_shape,) * (2 * core_count))(
        inputs, token_ids, cotangent
    )

    got = []
    for at, part in enumerate(col_parts):
        dy, dc = at // core_count, at % core_count
        if dy and dc:
            size = 2 * core_count
            perm = []
            for i in range(size):
                y, c = i // core_count, i % core_count
                perm.append((i, (y ^ 1) * core_count + (c + dc) % core_count))
            part = lax.ppermute(part, ("y", "c"), perm)
        elif dy:
            part = swap(part, "y")
        elif dc:
            part = rotate(part, "c", dc)
        got.append(part)

    starts = [sum(widths[:k]) for k in range(len(widths))]

    def several(count, width):
        return jax.ShapeDtypeStruct((seqs * count, length, width), bf)

    def many_rows(count):
        return jax.ShapeDtypeStruct((seqs * count, half, length), bf)

    z2 = swap(send, "zh")
    z1 = swap(keep, "zl")
    packs = [None] * len(widths)
    near, pass_on, own, other = call(
        gather_kernel, (many_rows(3), many_rows(1)) + (several(2 * core_count, widths[0]),) * 2
    )(keep, z1, z2, *got)
    packs[0] = [own, other]
    pack_shapes = [several(2 * core_count, width) for width in widths[1:] for _ in range(2)]
    own_rows, far, *others = call(
        functools.partial(second_kernel, starts[1:]), (many_rows(4), many_rows(1)) + tuple(pack_shapes)
    )(near, swap(pass_on, "zl"), *got)
    for k in range(1, len(widths)):
        packs[k] = others[2 * k - 2 : 2 * k]
    from_zh = swap(packs[0][0], "zh")
    from_zl = swap(packs[0][1], "zl")
    from_both = swap(packs[0][1], ("zh", "zl"))
    first_cols = [packs[0][0], from_zl, from_zh, from_both]
    all_rows = call(third_kernel, many_rows(8))(
        own_rows, swap(near, "y"), swap(far, "y"), after=[from_zh, from_zl, from_both] + other_weights[::2]
    )
    rows = [rotate(all_rows, "c", dc) if dc else all_rows for dc in range(core_count)]
    places = []
    for dz in range(4):
        for dy in range(2):
            for dc in range(core_count):
                for s in range(seqs):
                    places.append((dc, (dy * 4 + dz) * seqs + s, dz, (dy * core_count + dc) * seqs + s))

    chunks = []
    for k, width in enumerate(widths):
        own, other = packs[k]
        cols = [own, swap(other, "zl"), swap(own, "zh"), swap(other, ("zh", "zl"))] if k else first_cols
        last = k == len(widths) - 1
        code_shape = jax.ShapeDtypeStruct((span, width), jnp.int16)
        four_shape = jax.ShapeDtypeStruct((4, span, width), jnp.int16)
        outs = call(
            functools.partial(fisher_kernel, places, len(rows), 1.0 / (length * total_seqs), code_scale),
            (code_shape,) * 4 if last else (four_shape,),
            [pltpu.VMEM((half, width), jnp.float32)],
            flops=2 * half * width * length * total_seqs,
            bytes_accessed=2 * length * total_seqs * (half + width),
        )(*rows, *cols)
        if not last:
            from_models = [rotate(outs[0], "mp", offset) for offset in range(1, models)]
            parts = call(
                functools.partial(models_kernel, models),
                (jax.ShapeDtypeStruct((models, span, width), jnp.int16),) * 4,
            )(outs[0], *from_models, after=other_weights[1::2])
            parts = [parts[0], swap(parts[1], "y"), swap(parts[2], "zl"), swap(parts[3], ("zl", "y"))]
            chunks += parts
        else:
            codes = call(code_kernel, four_shape)(
                outs[0],
                swap(outs[1], "y"),
                swap(outs[2], "zl"),
                swap(outs[3], ("zl", "y")),
                after=() if k else other_weights[1::2],
            )
            all_codes = [codes] + [rotate(codes, "mp", offset) for offset in range(1, models)]
    early = call(
        functools.partial(early_merge_kernel, models, tile_width, starts[-1], widths[-1], code_scale),
        jax.ShapeDtypeStruct((4, span, widths[-1]), jnp.float32),
    )(weights, *other_weights, *all_codes)
    operands = [early, weights, *other_weights, *chunks]
    result = pl.pallas_call(
        functools.partial(last_merge_kernel, models, tile_width, starts, widths, code_scale),
        out_shape=jax.ShapeDtypeStruct(weights.shape, jnp.float32),
        in_specs=[VMEM] * len(operands),
        out_specs=pl.BlockSpec(memory_space=pltpu.HBM),
        scratch_shapes=[
            pltpu.VMEM((4, span, tile_width), jnp.float32),
            pltpu.SemaphoreType.DMA((4 * len(widths),)),
        ],
        compiler_params=pltpu.CompilerParams(vmem_limit_bytes=VMEM_LIMIT),
    )(*operands)
    return result[None]


def solution(mesh):
    models, devices = mesh.shape["mp"], mesh.shape["tok"]
    grid = Mesh(mesh.devices.reshape(models, 2, 2, ROW_BLOCKS // 4, devices // ROW_BLOCKS), ("mp",) + TOK)
    in_specs = (
        P("mp", TOK, None, None),
        P("mp", TOK, None, None),
        P("mp", TOK, None),
        P("mp", TOK, None, None),
    )
    return jax.shard_map(shards, mesh=grid, in_specs=in_specs, out_specs=P(TOK, None, None), check_vma=False)
```

```python
import functools
import math

import jax
import jax.numpy as jnp
from jax import lax
from jax.experimental import pallas as pl
from jax.experimental.pallas import tpu as pltpu
from jax.sharding import Mesh
from jax.sharding import PartitionSpec as P

ROW_BLOCKS = 8
FIRST_TEXT = 37984
LARGEST = 6.0

damping = 0.1

TOK = ("zh", "zl", "y", "c")
VMEM = pl.BlockSpec(memory_space=pltpu.VMEM)
VMEM_LIMIT = 28 * 1024 * 1024

CHUNKS = (0.5, 0.5)


def swap(value, axes):
    if isinstance(axes, str):
        return lax.ppermute(value, axes, [(0, 1), (1, 0)])
    return lax.ppermute(value, axes, [(i, i ^ 3) for i in range(4)])


def rotate(value, axis, offset):
    size = lax.axis_size(axis)
    return lax.ppermute(value, axis, [(i, (i + offset) % size) for i in range(size)])


def call(body, out_shape, scratch_shapes=(), flops=0, bytes_accessed=0):
    def run(*args, after=()):
        def kernel(*refs):
            body(*refs[: len(args)], *refs[len(args) + len(after) :])

        return pl.pallas_call(
            kernel,
            out_shape=out_shape,
            in_specs=[VMEM] * len(args) + [pl.BlockSpec(memory_space=pl.ANY)] * len(after),
            out_specs=jax.tree.map(lambda _: VMEM, out_shape),
            scratch_shapes=list(scratch_shapes),
            compiler_params=pltpu.CompilerParams(vmem_limit_bytes=VMEM_LIMIT),
            cost_estimate=pl.CostEstimate(flops=flops, bytes_accessed=bytes_accessed, transcendentals=0),
        )(*args, *after)

    return run


def front_kernel(inputs_ref, ids_ref, cot_ref, keep_ref, send_ref, *outs):
    half = keep_ref.shape[1]
    own = lax.axis_index("zh")
    for ref, part in ((keep_ref, own), (send_ref, 1 - own)):
        for s in range(inputs_ref.shape[0]):
            start = pl.multiple_of(part * half, half)
            ref[s] = inputs_ref[s, :, pl.ds(start, half)].T
    seqs, length, width = ids_ref.shape[0], cot_ref.shape[1], outs[0].shape[3]
    core_count = len(outs) // 2
    own_y, own_c = lax.axis_index("y"), lax.axis_index("c")
    for s in range(seqs):
        kept = jnp.broadcast_to((ids_ref[s : s + 1, :] >= FIRST_TEXT).astype(jnp.float32), (128, length)).T
        kept = kept[:, :1] > 0.5
        for at, ref in enumerate(outs):
            to_y = own_y ^ (at // core_count)
            to_c = lax.rem(own_c + at % core_count, core_count)
            for zl in range(2):
                start = pl.multiple_of(((to_c * 2 + zl) * 2 + to_y) * width, width)
                piece = cot_ref[s, :, pl.ds(start, width)]
                ref[zl, s] = jnp.where(kept, piece, jnp.zeros_like(piece))


def fill(out, *refs):
    at = 0
    for ref in refs:
        out[at : at + ref.shape[0]] = ref[...]
        at += ref.shape[0]


def pack(start, own_ref, other_ref, sources):
    own, width = lax.axis_index("zl"), other_ref.shape[2]
    for which, ref in enumerate((own_ref, other_ref)):
        for i, source in enumerate(sources):
            seqs = source.shape[1]
            ref[i * seqs : (i + 1) * seqs] = source[own ^ which, :, :, start : start + width]


def gather_kernel(keep, z1, z2, *refs):
    near, pass_on, own_ref, other_ref = refs[-4:]
    fill(near, keep, z1, z2)
    fill(pass_on, z2)
    pack(0, own_ref, other_ref, refs[:-4])


def second_kernel(starts, near, z3, *refs):
    count = 2 + 2 * len(starts)
    sources, (own_rows, far, *outs) = refs[:-count], refs[-count:]
    fill(far, z3)
    fill(own_rows, near, z3)
    for k, start in enumerate(starts):
        pack(start, outs[2 * k], outs[2 * k + 1], sources)


def third_kernel(own, first, second, out):
    fill(out, own, first, second)


def code_kernel(*refs):
    for at, ref in enumerate(refs[:-1]):
        refs[-1][at] = ref[...]


def fisher_kernel(places, row_count, scale, code_scale, *refs):
    rows, cols, outs, total = refs[:row_count], refs[row_count : row_count + 4], refs[row_count + 4 : -1], refs[-1]
    span = total.shape[0] // 4
    own_zl, own_y = lax.axis_index("zl"), lax.axis_index("y")

    for group in range(4):
        part = slice(group * span, (group + 1) * span)
        acc = None
        for row_at, row_sub, col_at, col_sub in places:
            g = jnp.dot(rows[row_at][row_sub, part, :], cols[col_at][col_sub], preferred_element_type=jnp.float32)
            acc = g * g if acc is None else acc + g * g
        damped = acc * scale + damping
        code = jnp.round((jnp.log(damped) - math.log(damping)) * code_scale) - 32768.0
        total[part, :] = jnp.clip(code, -32768.0, 32767.0)
    for at in range(4):
        group = (own_zl ^ (at // 2)) * 2 + (own_y ^ (at % 2))
        start = pl.multiple_of(group * span, span)
        code = total[pl.ds(start, span), :].astype(jnp.int32).astype(jnp.int16)
        if len(outs) == 1:
            outs[0][at] = code
        else:
            outs[at][...] = code


def models_kernel(models, *refs):
    for at, out in enumerate(refs[models:]):
        for m in range(models):
            out[m] = refs[m][at]


def merge_chunk(senders, models, tile_width, first, width, code_scale, weights, codes, store):
    own_zl, own_y, own_m = lax.axis_index("zl"), lax.axis_index("y"), lax.axis_index("mp")

    def pick(values, j):
        chosen = values[0]
        for offset in range(1, models):
            chosen = jnp.where(lax.rem(own_m + models - offset, models) == j, values[offset], chosen)
        return chosen

    for at in senders:
        sub = (own_zl ^ (at // 2)) * 2 + (own_y ^ (at % 2))
        start = pl.multiple_of(sub * tile_width + first, 128)
        codes_here = [codes(m, at).astype(jnp.int32) for m in range(models)]
        weights_here = [weights[0][:, pl.ds(start, width)]]
        for m in range(1, models):
            halves = [half[:, pl.ds(start, width)] for half in weights[2 * m - 1 : 2 * m + 1]]
            weights_here.append(jnp.concatenate(halves, axis=0))
        base = pick(codes_here, 0)
        num, den = pick(weights_here, 0), None
        for j in range(1, models):
            ratio = jnp.exp((pick(codes_here, j) - base).astype(jnp.float32) * (1.0 / code_scale))
            num = num + ratio * pick(weights_here, j)
            den = 1.0 + ratio if den is None else den + ratio
        store(at, start, num if den is None else num / den)


def early_merge_kernel(models, tile_width, first, width, code_scale, *refs):
    def store(at, start, value):
        refs[-1][at] = value

    weights, codes = refs[: 2 * models - 1], refs[2 * models - 1 : -1]
    merge_chunk(range(4), models, tile_width, first, width, code_scale, weights, lambda m, at: codes[m][at], store)


def near_merge_kernel(models, tile_width, first, width, code_scale, *refs):
    def store(at, start, value):
        refs[-1][at] = value

    weights, codes = refs[: 2 * models - 1], refs[2 * models - 1 : -1]
    merge_chunk(range(2), models, tile_width, first, width, code_scale, weights, lambda m, at: codes[at][m], store)


def last_merge_kernel(models, tile_width, firsts, widths, code_scale, *refs):
    count = len(widths) - 1
    last, nears, refs = refs[0], refs[1 : 1 + count], refs[1 + count :]
    weights, codes, (out, parts, done) = refs[: 2 * models - 1], refs[2 * models - 1 : -3], refs[-3:]
    own_zl, own_y = lax.axis_index("zl"), lax.axis_index("y")
    copies = []

    def send(source, start, width):
        copies.append(pltpu.make_async_copy(source, out.at[:, pl.ds(start, width)], done.at[len(copies)]))
        copies[-1].start()

    for ref, first, width, senders in zip((last, *nears), (firsts[-1], *firsts), (widths[-1], *widths), (4, 2, 2, 2)):
        for at in range(senders):
            sub = (own_zl ^ (at // 2)) * 2 + (own_y ^ (at % 2))
            send(ref.at[at], pl.multiple_of(sub * tile_width + first, 128), width)
    for k in range(count):
        first, width = firsts[k], widths[k]

        def store(at, start, value):
            parts[at - 2, :, first : first + width] = value
            send(parts.at[at - 2, :, pl.ds(first, width)], start, width)

        here = codes[2 * k : 2 * k + 2]
        merge_chunk(
            range(2, 4), models, tile_width, first, width, code_scale, weights, lambda m, at: here[at - 2][m], store
        )
    for copy in copies:
        copy.wait()


def shards(inputs, cotangent, token_ids, weights):
    models = lax.axis_size("mp")
    core_count = lax.axis_size("c")
    inputs, cotangent, token_ids, weights = inputs[0], cotangent[0], token_ids[0], weights[0, 0]
    seqs, length, feature_width = inputs.shape
    query_width = cotangent.shape[2]
    bf = jnp.bfloat16
    half = feature_width // 2
    tile_width = query_width // (4 * core_count)
    span = half // 4
    total_seqs = seqs * 8 * core_count
    widths = [int(tile_width * part) for part in CHUNKS]
    if any(width % 128 for width in widths):
        widths = [tile_width]
    peak = LARGEST**4 * length + damping
    code_scale = 65535.0 / (math.log(peak) - math.log(damping))

    early_rows = weights.shape[0] // 2
    other_weights = []
    for offset in range(1, models):
        other_weights += [rotate(weights[:early_rows], "mp", offset), rotate(weights[early_rows:], "mp", offset)]

    col_shape = jax.ShapeDtypeStruct((2, seqs, length, tile_width), bf)
    row_shape = jax.ShapeDtypeStruct((seqs, half, length), bf)
    keep, send, *col_parts = call(front_kernel, (row_shape,) * 2 + (col_shape,) * (2 * core_count))(
        inputs, token_ids, cotangent
    )

    got = []
    for at, part in enumerate(col_parts):
        dy, dc = at // core_count, at % core_count
        if dy and dc:
            size = 2 * core_count
            perm = []
            for i in range(size):
                y, c = i // core_count, i % core_count
                perm.append((i, (y ^ 1) * core_count + (c + dc) % core_count))
            part = lax.ppermute(part, ("y", "c"), perm)
        elif dy:
            part = swap(part, "y")
        elif dc:
            part = rotate(part, "c", dc)
        got.append(part)

    starts = [sum(widths[:k]) for k in range(len(widths))]

    def several(count, width):
        return jax.ShapeDtypeStruct((seqs * count, length, width), bf)

    def many_rows(count):
        return jax.ShapeDtypeStruct((seqs * count, half, length), bf)

    z2 = swap(send, "zh")
    z1 = swap(keep, "zl")
    packs = [None] * len(widths)
    near, pass_on, own, other = call(
        gather_kernel, (many_rows(3), many_rows(1)) + (several(2 * core_count, widths[0]),) * 2
    )(keep, z1, z2, *got)
    packs[0] = [own, other]
    pack_shapes = [several(2 * core_count, width) for width in widths[1:] for _ in range(2)]
    own_rows, far, *others = call(
        functools.partial(second_kernel, starts[1:]), (many_rows(4), many_rows(1)) + tuple(pack_shapes)
    )(near, swap(pass_on, "zl"), *got)
    for k in range(1, len(widths)):
        packs[k] = others[2 * k - 2 : 2 * k]
    from_zh = swap(packs[0][0], "zh")
    from_zl = swap(packs[0][1], "zl")
    from_both = swap(packs[0][1], ("zh", "zl"))
    first_cols = [packs[0][0], from_zl, from_zh, from_both]
    all_rows = call(third_kernel, many_rows(8))(
        own_rows, swap(near, "y"), swap(far, "y"), after=[from_zh, from_zl, from_both] + other_weights[::2]
    )
    rows = [rotate(all_rows, "c", dc) if dc else all_rows for dc in range(core_count)]
    places = []
    for dz in range(4):
        for dy in range(2):
            for dc in range(core_count):
                for s in range(seqs):
                    places.append((dc, (dy * 4 + dz) * seqs + s, dz, (dy * core_count + dc) * seqs + s))

    nears, chunks = [], []
    for k, width in enumerate(widths):
        own, other = packs[k]
        cols = [own, swap(other, "zl"), swap(own, "zh"), swap(other, ("zh", "zl"))] if k else first_cols
        last = k == len(widths) - 1
        code_shape = jax.ShapeDtypeStruct((span, width), jnp.int16)
        four_shape = jax.ShapeDtypeStruct((4, span, width), jnp.int16)
        outs = call(
            functools.partial(fisher_kernel, places, len(rows), 1.0 / (length * total_seqs), code_scale),
            (code_shape,) * 4 if last else (four_shape,),
            [pltpu.VMEM((half, width), jnp.float32)],
            flops=2 * half * width * length * total_seqs,
            bytes_accessed=2 * length * total_seqs * (half + width),
        )(*rows, *cols)
        if not last:
            from_models = [rotate(outs[0], "mp", offset) for offset in range(1, models)]
            parts = call(
                functools.partial(models_kernel, models),
                (jax.ShapeDtypeStruct((models, span, width), jnp.int16),) * 4,
            )(outs[0], *from_models, after=other_weights[1::2])
            parts = [parts[0], swap(parts[1], "y"), swap(parts[2], "zl"), swap(parts[3], ("zl", "y"))]
            nears.append(
                call(
                    functools.partial(near_merge_kernel, models, tile_width, starts[k], width, code_scale),
                    jax.ShapeDtypeStruct((2, span, width), jnp.float32),
                )(weights, *other_weights, *parts[:2])
            )
            chunks += parts[2:]
        else:
            far = swap(outs[3], ("zl", "y"))
            over_z = swap(outs[2], "zl")
            over_y = swap(outs[1], "y")
            codes = call(code_kernel, four_shape)(
                outs[0],
                over_y,
                over_z,
                far,
                after=() if k else other_weights[1::2],
            )
            all_codes = [codes] + [rotate(codes, "mp", offset) for offset in range(1, models)]
    early = call(
        functools.partial(early_merge_kernel, models, tile_width, starts[-1], widths[-1], code_scale),
        jax.ShapeDtypeStruct((4, span, widths[-1]), jnp.float32),
    )(weights, *other_weights, *all_codes, after=nears)
    operands = [early, *nears, weights, *other_weights, *chunks]
    result = pl.pallas_call(
        functools.partial(last_merge_kernel, models, tile_width, starts, widths, code_scale),
        out_shape=jax.ShapeDtypeStruct(weights.shape, jnp.float32),
        in_specs=[VMEM] * len(operands),
        out_specs=pl.BlockSpec(memory_space=pltpu.HBM),
        scratch_shapes=[
            pltpu.VMEM((2, span, tile_width), jnp.float32),
            pltpu.SemaphoreType.DMA((4 * len(widths),)),
        ],
        compiler_params=pltpu.CompilerParams(vmem_limit_bytes=VMEM_LIMIT),
    )(*operands)
    return result[None]


def solution(mesh):
    models, devices = mesh.shape["mp"], mesh.shape["tok"]
    grid = Mesh(mesh.devices.reshape(models, 2, 2, ROW_BLOCKS // 4, devices // ROW_BLOCKS), ("mp",) + TOK)
    in_specs = (
        P("mp", TOK, None, None),
        P("mp", TOK, None, None),
        P("mp", TOK, None),
        P("mp", TOK, None, None),
    )
    return jax.shard_map(shards, mesh=grid, in_specs=in_specs, out_specs=P(TOK, None, None), check_vma=False)
```

```python
import functools
import math

import jax
import jax.numpy as jnp
from jax import lax
from jax.experimental import pallas as pl
from jax.experimental.pallas import tpu as pltpu
from jax.sharding import Mesh
from jax.sharding import PartitionSpec as P

ROW_BLOCKS = 8
FIRST_TEXT = 37984
LARGEST = 6.0

damping = 0.1

TOK = ("zh", "zl", "y", "c")
VMEM = pl.BlockSpec(memory_space=pltpu.VMEM)
VMEM_LIMIT = 28 * 1024 * 1024

CHUNKS = (0.5, 0.5)


def swap(value, axes):
    if isinstance(axes, str):
        return lax.ppermute(value, axes, [(0, 1), (1, 0)])
    return lax.ppermute(value, axes, [(i, i ^ 3) for i in range(4)])


def rotate(value, axis, offset):
    size = lax.axis_size(axis)
    return lax.ppermute(value, axis, [(i, (i + offset) % size) for i in range(size)])


def call(body, out_shape, scratch_shapes=(), flops=0, bytes_accessed=0):
    def run(*args, after=()):
        def kernel(*refs):
            body(*refs[: len(args)], *refs[len(args) + len(after) :])

        return pl.pallas_call(
            kernel,
            out_shape=out_shape,
            in_specs=[VMEM] * len(args) + [pl.BlockSpec(memory_space=pl.ANY)] * len(after),
            out_specs=jax.tree.map(lambda _: VMEM, out_shape),
            scratch_shapes=list(scratch_shapes),
            compiler_params=pltpu.CompilerParams(vmem_limit_bytes=VMEM_LIMIT),
            cost_estimate=pl.CostEstimate(flops=flops, bytes_accessed=bytes_accessed, transcendentals=0),
        )(*args, *after)

    return run


def front_kernel(inputs_ref, ids_ref, cot_ref, keep_ref, send_ref, *outs):
    half = keep_ref.shape[1]
    own = lax.axis_index("zh")
    for ref, part in ((keep_ref, own), (send_ref, 1 - own)):
        for s in range(inputs_ref.shape[0]):
            start = pl.multiple_of(part * half, half)
            ref[s] = inputs_ref[s, :, pl.ds(start, half)].T
    core_count, _, seqs, length, width = outs[0].shape
    own_y, own_c = lax.axis_index("y"), lax.axis_index("c")
    for s in range(seqs):
        kept = jnp.broadcast_to((ids_ref[s : s + 1, :] >= FIRST_TEXT).astype(jnp.float32), (128, length)).T
        kept = kept[:, :1] > 0.5
        for dy, ref in enumerate(outs):
            for dc in range(core_count):
                to_c = lax.rem(own_c + dc, core_count)
                for zl in range(2):
                    start = pl.multiple_of(((to_c * 2 + zl) * 2 + (own_y ^ dy)) * width, width)
                    piece = cot_ref[s, :, pl.ds(start, width)]
                    ref[dc, zl, s] = jnp.where(kept, piece, jnp.zeros_like(piece))


def core_kernel(here, there, *outs):
    for at, out in enumerate(outs):
        out[0] = here[at]
        out[1] = there[at]


def fill(out, *refs):
    at = 0
    for ref in refs:
        out[at : at + ref.shape[0]] = ref[...]
        at += ref.shape[0]


def pack(start, own_ref, other_ref, sources):
    own, width, seqs = lax.axis_index("zl"), other_ref.shape[2], sources[0].shape[2]
    for which, ref in enumerate((own_ref, other_ref)):
        at = 0
        for dy in range(2):
            for source in sources:
                ref[at : at + seqs] = source[dy, own ^ which, :, :, start : start + width]
                at += seqs


def gather_kernel(keep, z1, z2, *refs):
    near, pass_on, own_ref, other_ref = refs[-4:]
    fill(near, keep, z1, z2)
    fill(pass_on, z2)
    pack(0, own_ref, other_ref, refs[:-4])


def second_kernel(starts, near, z3, *refs):
    count = 2 + 2 * len(starts)
    sources, (own_rows, far, *outs) = refs[:-count], refs[-count:]
    fill(far, z3)
    fill(own_rows, near, z3)
    for k, start in enumerate(starts):
        pack(start, outs[2 * k], outs[2 * k + 1], sources)


def third_kernel(own, first, second, out):
    fill(out, own, first, second)


def code_kernel(*refs):
    for at, ref in enumerate(refs[:-1]):
        refs[-1][at] = ref[...]


def fisher_kernel(places, row_count, scale, code_scale, *refs):
    rows, cols, outs, total = refs[:row_count], refs[row_count : row_count + 4], refs[row_count + 4 : -1], refs[-1]
    span = total.shape[0] // 4
    own_zl, own_y = lax.axis_index("zl"), lax.axis_index("y")

    for group in range(4):
        part = slice(group * span, (group + 1) * span)
        acc = None
        for row_at, row_sub, col_at, col_sub in places:
            g = jnp.dot(rows[row_at][row_sub, part, :], cols[col_at][col_sub], preferred_element_type=jnp.float32)
            acc = g * g if acc is None else acc + g * g
        damped = acc * scale + damping
        code = jnp.round((jnp.log(damped) - math.log(damping)) * code_scale) - 32768.0
        total[part, :] = jnp.clip(code, -32768.0, 32767.0)
    for at in range(4):
        group = (own_zl ^ (at // 2)) * 2 + (own_y ^ (at % 2))
        start = pl.multiple_of(group * span, span)
        code = total[pl.ds(start, span), :].astype(jnp.int32).astype(jnp.int16)
        if len(outs) == 1:
            outs[0][at] = code
        else:
            outs[at][...] = code


def pick(values, j):
    own, models = lax.axis_index("mp"), len(values)
    chosen = values[0]
    for offset in range(1, models):
        chosen = jnp.where(lax.rem(own + models - offset, models) == j, values[offset], chosen)
    return chosen


def code_steps(codes, j):
    whole = [code.astype(jnp.int32) for code in codes]
    return (pick(whole, j) - pick(whole, 0)).astype(jnp.float32)


def steps_kernel(models, *refs):
    for at, out in enumerate(refs[models:]):
        for j in range(1, models):
            steps = jnp.round(code_steps([ref[at] for ref in refs[:models]], j) * 0.5)
            out[j - 1] = jnp.clip(steps, -32768.0, 32767.0).astype(jnp.int32).astype(jnp.int16)


def merge_chunk(senders, models, tile_width, first, width, code_scale, weights, steps, store):
    own_zl, own_y = lax.axis_index("zl"), lax.axis_index("y")
    for at in senders:
        sub = (own_zl ^ (at // 2)) * 2 + (own_y ^ (at % 2))
        start = pl.multiple_of(sub * tile_width + first, 128)
        weights_here = [weight[:, pl.ds(start, width)] for weight in weights]
        num, den = pick(weights_here, 0), None
        for j in range(1, models):
            ratio = jnp.exp(steps(at, j) * (1.0 / code_scale))
            num = num + ratio * pick(weights_here, j)
            den = 1.0 + ratio if den is None else den + ratio
        store(at, start, num if den is None else num / den)


def two_steps(value):
    return value.astype(jnp.int32).astype(jnp.float32) * 2.0


def early_merge_kernel(models, tile_width, first, width, code_scale, *refs):
    def store(at, start, value):
        refs[-1][at] = value

    weights, codes = refs[:models], refs[models:-1]
    merge_chunk(range(4), models, tile_width, first, width, code_scale, weights, lambda at, j: code_steps([code[at] for code in codes], j), store)


def near_merge_kernel(models, tile_width, first, width, code_scale, *refs):
    def store(at, start, value):
        refs[-1][at] = value

    weights, codes = refs[:models], refs[models:-1]
    merge_chunk(range(2), models, tile_width, first, width, code_scale, weights, lambda at, j: two_steps(codes[at][j - 1]), store)


def last_merge_kernel(models, tile_width, firsts, widths, code_scale, *refs):
    count = len(widths) - 1
    last, nears, refs = refs[0], refs[1 : 1 + count], refs[1 + count :]
    weights, codes, (out, parts, done) = refs[:models], refs[models:-3], refs[-3:]
    own_zl, own_y = lax.axis_index("zl"), lax.axis_index("y")
    copies = []

    def send(source, start, width):
        copies.append(pltpu.make_async_copy(source, out.at[:, pl.ds(start, width)], done.at[len(copies)]))
        copies[-1].start()

    for ref, first, width, senders in zip((last, *nears), (firsts[-1], *firsts), (widths[-1], *widths), (4, 2, 2, 2)):
        for at in range(senders):
            sub = (own_zl ^ (at // 2)) * 2 + (own_y ^ (at % 2))
            send(ref.at[at], pl.multiple_of(sub * tile_width + first, 128), width)
    for k in range(count):
        first, width = firsts[k], widths[k]

        def store(at, start, value):
            parts[at - 2, :, first : first + width] = value
            send(parts.at[at - 2, :, pl.ds(first, width)], start, width)

        here = codes[2 * k : 2 * k + 2]
        merge_chunk(
            range(2, 4), models, tile_width, first, width, code_scale, weights, lambda at, j: two_steps(here[at - 2][j - 1]), store
        )
    for copy in copies:
        copy.wait()


def shards(inputs, cotangent, token_ids, weights):
    models = lax.axis_size("mp")
    core_count = lax.axis_size("c")
    inputs, cotangent, token_ids, weights = inputs[0], cotangent[0], token_ids[0], weights[0, 0]
    seqs, length, feature_width = inputs.shape
    query_width = cotangent.shape[2]
    bf = jnp.bfloat16
    half = feature_width // 2
    tile_width = query_width // (4 * core_count)
    span = half // 4
    total_seqs = seqs * 8 * core_count
    widths = [int(tile_width * part) for part in CHUNKS]
    if any(width % 128 for width in widths):
        widths = [tile_width]
    peak = LARGEST**4 * length + damping
    code_scale = 65535.0 / (math.log(peak) - math.log(damping))

    other_weights = [rotate(weights, "mp", offset) for offset in range(1, models)]
    col_shape = jax.ShapeDtypeStruct((core_count, 2, seqs, length, tile_width), bf)
    row_shape = jax.ShapeDtypeStruct((seqs, half, length), bf)
    keep, send, here, there = call(front_kernel, (row_shape, row_shape, col_shape, col_shape))(
        inputs, token_ids, cotangent
    )

    starts = [sum(widths[:k]) for k in range(len(widths))]

    def several(count, width):
        return jax.ShapeDtypeStruct((seqs * count, length, width), bf)

    def many_rows(count):
        return jax.ShapeDtypeStruct((seqs * count, half, length), bf)

    z2 = swap(send, "zh")
    z1 = swap(keep, "zl")
    pair_shape = jax.ShapeDtypeStruct((2, 2, seqs, length, tile_width), bf)
    got = call(core_kernel, (pair_shape,) * core_count)(here, swap(there, "y"), after=[z1, z2])
    got = [rotate(part, "c", dc) if dc else part for dc, part in enumerate(got)]
    packs = [None] * len(widths)
    near, pass_on, own, other = call(
        gather_kernel, (many_rows(3), many_rows(1)) + (several(2 * core_count, widths[0]),) * 2
    )(keep, z1, z2, *got)
    packs[0] = [own, other]
    pack_shapes = [several(2 * core_count, width) for width in widths[1:] for _ in range(2)]
    own_rows, far, *others = call(
        functools.partial(second_kernel, starts[1:]), (many_rows(4), many_rows(1)) + tuple(pack_shapes)
    )(near, swap(pass_on, "zl"), *got)
    for k in range(1, len(widths)):
        packs[k] = others[2 * k - 2 : 2 * k]
    from_zh = swap(packs[0][0], "zh")
    from_zl = swap(packs[0][1], "zl")
    from_both = swap(packs[0][1], ("zh", "zl"))
    first_cols = [packs[0][0], from_zl, from_zh, from_both]
    all_rows = call(third_kernel, many_rows(8))(
        own_rows, swap(near, "y"), swap(far, "y"), after=[from_zh, from_zl, from_both] + other_weights
    )
    rows = [rotate(all_rows, "c", dc) if dc else all_rows for dc in range(core_count)]
    places = []
    for dz in range(4):
        for dy in range(2):
            for dc in range(core_count):
                for s in range(seqs):
                    places.append((dc, (dy * 4 + dz) * seqs + s, dz, (dy * core_count + dc) * seqs + s))

    nears, chunks = [], []
    for k, width in enumerate(widths):
        own, other = packs[k]
        cols = [own, swap(other, "zl"), swap(own, "zh"), swap(other, ("zh", "zl"))] if k else first_cols
        last = k == len(widths) - 1
        code_shape = jax.ShapeDtypeStruct((span, width), jnp.int16)
        four_shape = jax.ShapeDtypeStruct((4, span, width), jnp.int16)
        outs = call(
            functools.partial(fisher_kernel, places, len(rows), 1.0 / (length * total_seqs), code_scale),
            (code_shape,) * 4 if last else (four_shape,),
            [pltpu.VMEM((half, width), jnp.float32)],
            flops=2 * half * width * length * total_seqs,
            bytes_accessed=2 * length * total_seqs * (half + width),
        )(*rows, *cols)
        if not last:
            from_models = [rotate(outs[0], "mp", offset) for offset in range(1, models)]
            parts = call(
                functools.partial(steps_kernel, models),
                (jax.ShapeDtypeStruct((models - 1, span, width), jnp.int16),) * 4,
            )(outs[0], *from_models, after=other_weights)
            parts = [parts[0], swap(parts[1], "y"), swap(parts[2], "zl"), swap(parts[3], ("zl", "y"))]
            nears.append(
                call(
                    functools.partial(near_merge_kernel, models, tile_width, starts[k], width, code_scale),
                    jax.ShapeDtypeStruct((2, span, width), jnp.float32),
                )(weights, *other_weights, *parts[:2])
            )
            chunks += parts[2:]
        else:
            far = swap(outs[3], ("zl", "y"))
            over_z = swap(outs[2], "zl")
            over_y = swap(outs[1], "y")
            codes = call(code_kernel, four_shape)(
                outs[0],
                over_y,
                over_z,
                far,
                after=() if k else other_weights,
            )
            all_codes = [codes] + [rotate(codes, "mp", offset) for offset in range(1, models)]
    early = call(
        functools.partial(early_merge_kernel, models, tile_width, starts[-1], widths[-1], code_scale),
        jax.ShapeDtypeStruct((4, span, widths[-1]), jnp.float32),
    )(weights, *other_weights, *all_codes, after=nears)
    operands = [early, *nears, weights, *other_weights, *chunks]
    result = pl.pallas_call(
        functools.partial(last_merge_kernel, models, tile_width, starts, widths, code_scale),
        out_shape=jax.ShapeDtypeStruct(weights.shape, jnp.float32),
        in_specs=[VMEM] * len(operands),
        out_specs=pl.BlockSpec(memory_space=pltpu.HBM),
        scratch_shapes=[
            pltpu.VMEM((2, span, tile_width), jnp.float32),
            pltpu.SemaphoreType.DMA((4 * len(widths),)),
        ],
        compiler_params=pltpu.CompilerParams(vmem_limit_bytes=VMEM_LIMIT),
    )(*operands)
    return result[None]


def solution(mesh):
    models, devices = mesh.shape["mp"], mesh.shape["tok"]
    grid = Mesh(mesh.devices.reshape(models, 2, 2, ROW_BLOCKS // 4, devices // ROW_BLOCKS), ("mp",) + TOK)
    in_specs = (
        P("mp", TOK, None, None),
        P("mp", TOK, None, None),
        P("mp", TOK, None),
        P("mp", TOK, None, None),
    )
    return jax.shard_map(shards, mesh=grid, in_specs=in_specs, out_specs=P(TOK, None, None), check_vma=False)
```

```python
import functools
import math

import jax
import jax.numpy as jnp
from jax import lax
from jax.experimental import pallas as pl
from jax.experimental.pallas import tpu as pltpu
from jax.sharding import Mesh
from jax.sharding import PartitionSpec as P

ROW_BLOCKS = 8
FIRST_TEXT = 37984
LARGEST = 6.0

damping = 0.1

TOK = ("zh", "zl", "y", "c")
VMEM = pl.BlockSpec(memory_space=pltpu.VMEM)
VMEM_LIMIT = 28 * 1024 * 1024

CHUNKS = (0.5, 0.5)


def swap(value, axes):
    if isinstance(axes, str):
        return lax.ppermute(value, axes, [(0, 1), (1, 0)])
    return lax.ppermute(value, axes, [(i, i ^ 3) for i in range(4)])


def rotate(value, axis, offset):
    size = lax.axis_size(axis)
    return lax.ppermute(value, axis, [(i, (i + offset) % size) for i in range(size)])


def call(body, out_shape, scratch_shapes=(), flops=0, bytes_accessed=0):
    def run(*args, after=()):
        def kernel(*refs):
            body(*refs[: len(args)], *refs[len(args) + len(after) :])

        return pl.pallas_call(
            kernel,
            out_shape=out_shape,
            in_specs=[VMEM] * len(args) + [pl.BlockSpec(memory_space=pl.ANY)] * len(after),
            out_specs=jax.tree.map(lambda _: VMEM, out_shape),
            scratch_shapes=list(scratch_shapes),
            compiler_params=pltpu.CompilerParams(vmem_limit_bytes=VMEM_LIMIT),
            cost_estimate=pl.CostEstimate(flops=flops, bytes_accessed=bytes_accessed, transcendentals=0),
        )(*args, *after)

    return run


def front_kernel(inputs_ref, ids_ref, cot_ref, keep_ref, send_ref, *outs):
    half = keep_ref.shape[1]
    own = lax.axis_index("zh")
    for ref, part in ((keep_ref, own), (send_ref, 1 - own)):
        for s in range(inputs_ref.shape[0]):
            start = pl.multiple_of(part * half, half)
            ref[s] = inputs_ref[s, :, pl.ds(start, half)].T
    core_count, _, seqs, length, width = outs[0].shape
    own_y, own_c = lax.axis_index("y"), lax.axis_index("c")
    for s in range(seqs):
        kept = jnp.broadcast_to((ids_ref[s : s + 1, :] >= FIRST_TEXT).astype(jnp.float32), (128, length)).T
        kept = kept[:, :1] > 0.5
        for dy, ref in enumerate(outs):
            for dc in range(core_count):
                to_c = lax.rem(own_c + dc, core_count)
                for zl in range(2):
                    start = pl.multiple_of(((to_c * 2 + zl) * 2 + (own_y ^ dy)) * width, width)
                    piece = cot_ref[s, :, pl.ds(start, width)]
                    ref[dc, zl, s] = jnp.where(kept, piece, jnp.zeros_like(piece))


def core_kernel(here, there, *outs):
    for at, out in enumerate(outs):
        out[0] = here[at]
        out[1] = there[at]


def fill(out, *refs):
    at = 0
    for ref in refs:
        out[at : at + ref.shape[0]] = ref[...]
        at += ref.shape[0]


def pack(start, own_ref, other_ref, sources):
    own, width, seqs = lax.axis_index("zl"), other_ref.shape[2], sources[0].shape[2]
    for which, ref in enumerate((own_ref, other_ref)):
        at = 0
        for dy in range(2):
            for source in sources:
                ref[at : at + seqs] = source[dy, own ^ which, :, :, start : start + width]
                at += seqs


def gather_kernel(keep, z1, z2, *refs):
    near, pass_on, own_ref, other_ref = refs[-4:]
    fill(near, keep, z1, z2)
    fill(pass_on, z2)
    pack(0, own_ref, other_ref, refs[:-4])


def second_kernel(starts, near, z3, *refs):
    count = 2 + 2 * len(starts)
    sources, (own_rows, far, *outs) = refs[:-count], refs[-count:]
    fill(far, z3)
    fill(own_rows, near, z3)
    for k, start in enumerate(starts):
        pack(start, outs[2 * k], outs[2 * k + 1], sources)


def third_kernel(own, first, second, out):
    fill(out, own, first, second)


def code_kernel(*refs):
    for at, ref in enumerate(refs[:-1]):
        refs[-1][at] = ref[...]


def fisher_kernel(places, row_count, scale, code_scale, *refs):
    rows, cols, outs, total = refs[:row_count], refs[row_count : row_count + 4], refs[row_count + 4 : -1], refs[-1]
    span = total.shape[0] // 4
    own_zl, own_y = lax.axis_index("zl"), lax.axis_index("y")

    for group in range(4):
        part = slice(group * span, (group + 1) * span)
        acc = None
        for row_at, row_sub, col_at, col_sub in places:
            g = jnp.dot(rows[row_at][row_sub, part, :], cols[col_at][col_sub], preferred_element_type=jnp.float32)
            acc = g * g if acc is None else acc + g * g
        damped = acc * scale + damping
        code = jnp.round((jnp.log(damped) - math.log(damping)) * code_scale) - 32768.0
        total[part, :] = jnp.clip(code, -32768.0, 32767.0)
    for at in range(4):
        group = (own_zl ^ (at // 2)) * 2 + (own_y ^ (at % 2))
        start = pl.multiple_of(group * span, span)
        code = total[pl.ds(start, span), :].astype(jnp.int32).astype(jnp.int16)
        if len(outs) == 1:
            outs[0][at] = code
        else:
            outs[at][...] = code


def pick(values, j):
    own, models = lax.axis_index("mp"), len(values)
    chosen = values[0]
    for offset in range(1, models):
        chosen = jnp.where(lax.rem(own + models - offset, models) == j, values[offset], chosen)
    return chosen


def code_steps(codes, j):
    whole = [code.astype(jnp.int32) for code in codes]
    return (pick(whole, j) - pick(whole, 0)).astype(jnp.float32)


def steps_kernel(models, *refs):
    for at, out in enumerate(refs[models:]):
        for j in range(1, models):
            steps = jnp.round(code_steps([ref[at] for ref in refs[:models]], j) * 0.5)
            out[j - 1] = jnp.clip(steps, -32768.0, 32767.0).astype(jnp.int32).astype(jnp.int16)


def merge_chunk(senders, models, tile_width, first, width, code_scale, weights, steps, store):
    own_zl, own_y = lax.axis_index("zl"), lax.axis_index("y")
    for at in senders:
        sub = (own_zl ^ (at // 2)) * 2 + (own_y ^ (at % 2))
        start = pl.multiple_of(sub * tile_width + first, 128)
        weights_here = [weight[:, pl.ds(start, width)] for weight in weights]
        num, den = pick(weights_here, 0), None
        for j in range(1, models):
            ratio = jnp.exp(steps(at, j) * (1.0 / code_scale))
            num = num + ratio * pick(weights_here, j)
            den = 1.0 + ratio if den is None else den + ratio
        store(at, start, num if den is None else num / den)


def two_steps(value):
    return value.astype(jnp.int32).astype(jnp.float32) * 2.0


def early_merge_kernel(models, tile_width, first, width, code_scale, *refs):
    def store(at, start, value):
        refs[-1][at] = value

    weights, codes = refs[:models], refs[models:-1]

    def steps(at, j):
        return code_steps([codes[2 * m + 1][at - 1] if at else codes[2 * m][...] for m in range(models)], j)

    merge_chunk(range(4), models, tile_width, first, width, code_scale, weights, steps, store)


def near_merge_kernel(models, tile_width, first, width, code_scale, *refs):
    def store(at, start, value):
        refs[-1][at] = value

    weights, codes = refs[:models], refs[models:-1]
    merge_chunk(range(2), models, tile_width, first, width, code_scale, weights, lambda at, j: two_steps(codes[at][j - 1]), store)


def last_merge_kernel(models, tile_width, firsts, widths, code_scale, *refs):
    count = len(widths) - 1
    last, nears, refs = refs[0], refs[1 : 1 + count], refs[1 + count :]
    weights, codes, (out, parts, done) = refs[:models], refs[models:-3], refs[-3:]
    own_zl, own_y = lax.axis_index("zl"), lax.axis_index("y")
    copies = []

    def send(source, start, width):
        copies.append(pltpu.make_async_copy(source, out.at[:, pl.ds(start, width)], done.at[len(copies)]))
        copies[-1].start()

    for ref, first, width, senders in zip((last, *nears), (firsts[-1], *firsts), (widths[-1], *widths), (4, 2, 2, 2)):
        for at in range(senders):
            sub = (own_zl ^ (at // 2)) * 2 + (own_y ^ (at % 2))
            send(ref.at[at], pl.multiple_of(sub * tile_width + first, 128), width)
    for k in range(count):
        first, width = firsts[k], widths[k]

        def store(at, start, value):
            parts[at - 2, :, first : first + width] = value
            send(parts.at[at - 2, :, pl.ds(first, width)], start, width)

        here = codes[2 * k : 2 * k + 2]
        merge_chunk(
            range(2, 4), models, tile_width, first, width, code_scale, weights, lambda at, j: two_steps(here[at - 2][j - 1]), store
        )
    for copy in copies:
        copy.wait()


def shards(inputs, cotangent, token_ids, weights):
    models = lax.axis_size("mp")
    core_count = lax.axis_size("c")
    inputs, cotangent, token_ids, weights = inputs[0], cotangent[0], token_ids[0], weights[0, 0]
    seqs, length, feature_width = inputs.shape
    query_width = cotangent.shape[2]
    bf = jnp.bfloat16
    half = feature_width // 2
    tile_width = query_width // (4 * core_count)
    span = half // 4
    total_seqs = seqs * 8 * core_count
    widths = [int(tile_width * part) for part in CHUNKS]
    if any(width % 128 for width in widths):
        widths = [tile_width]
    peak = LARGEST**4 * length + damping
    code_scale = 65535.0 / (math.log(peak) - math.log(damping))

    other_weights = [rotate(weights, "mp", offset) for offset in range(1, models)]
    col_shape = jax.ShapeDtypeStruct((core_count, 2, seqs, length, tile_width), bf)
    row_shape = jax.ShapeDtypeStruct((seqs, half, length), bf)
    keep, send, here, there = call(front_kernel, (row_shape, row_shape, col_shape, col_shape))(
        inputs, token_ids, cotangent
    )

    starts = [sum(widths[:k]) for k in range(len(widths))]

    def several(count, width):
        return jax.ShapeDtypeStruct((seqs * count, length, width), bf)

    def many_rows(count):
        return jax.ShapeDtypeStruct((seqs * count, half, length), bf)

    z2 = swap(send, "zh")
    z1 = swap(keep, "zl")
    pair_shape = jax.ShapeDtypeStruct((2, 2, seqs, length, tile_width), bf)
    got = call(core_kernel, (pair_shape,) * core_count)(here, swap(there, "y"), after=[z1, z2])
    got = [rotate(part, "c", dc) if dc else part for dc, part in enumerate(got)]
    packs = [None] * len(widths)
    near, pass_on, own, other = call(
        gather_kernel, (many_rows(3), many_rows(1)) + (several(2 * core_count, widths[0]),) * 2
    )(keep, z1, z2, *got)
    packs[0] = [own, other]
    pack_shapes = [several(2 * core_count, width) for width in widths[1:] for _ in range(2)]
    own_rows, far, *others = call(
        functools.partial(second_kernel, starts[1:]), (many_rows(4), many_rows(1)) + tuple(pack_shapes)
    )(near, swap(pass_on, "zl"), *got)
    for k in range(1, len(widths)):
        packs[k] = others[2 * k - 2 : 2 * k]
    from_zh = swap(packs[0][0], "zh")
    from_zl = swap(packs[0][1], "zl")
    from_both = swap(packs[0][1], ("zh", "zl"))
    first_cols = [packs[0][0], from_zl, from_zh, from_both]
    all_rows = call(third_kernel, many_rows(8))(
        own_rows, swap(near, "y"), swap(far, "y"), after=[from_zh, from_zl, from_both] + other_weights
    )
    rows = [rotate(all_rows, "c", dc) if dc else all_rows for dc in range(core_count)]
    places = []
    for dz in range(4):
        for dy in range(2):
            for dc in range(core_count):
                for s in range(seqs):
                    places.append((dc, (dy * 4 + dz) * seqs + s, dz, (dy * core_count + dc) * seqs + s))

    nears, chunks = [], []
    for k, width in enumerate(widths):
        own, other = packs[k]
        cols = [own, swap(other, "zl"), swap(own, "zh"), swap(other, ("zh", "zl"))] if k else first_cols
        last = k == len(widths) - 1
        code_shape = jax.ShapeDtypeStruct((span, width), jnp.int16)
        four_shape = jax.ShapeDtypeStruct((4, span, width), jnp.int16)
        outs = call(
            functools.partial(fisher_kernel, places, len(rows), 1.0 / (length * total_seqs), code_scale),
            (code_shape,) * 4 if last else (four_shape,),
            [pltpu.VMEM((half, width), jnp.float32)],
            flops=2 * half * width * length * total_seqs,
            bytes_accessed=2 * length * total_seqs * (half + width),
        )(*rows, *cols)
        if not last:
            from_models = [rotate(outs[0], "mp", offset) for offset in range(1, models)]
            parts = call(
                functools.partial(steps_kernel, models),
                (jax.ShapeDtypeStruct((models - 1, span, width), jnp.int16),) * 4,
            )(outs[0], *from_models, after=other_weights)
            parts = [parts[0], swap(parts[1], "y"), swap(parts[2], "zl"), swap(parts[3], ("zl", "y"))]
            nears.append(
                call(
                    functools.partial(near_merge_kernel, models, tile_width, starts[k], width, code_scale),
                    jax.ShapeDtypeStruct((2, span, width), jnp.float32),
                )(weights, *other_weights, *parts[:2])
            )
            chunks += parts[2:]
        else:
            far = swap(outs[3], ("zl", "y"))
            over_z = swap(outs[2], "zl")
            over_y = swap(outs[1], "y")
            x_near = [rotate(outs[0], "mp", offset) for offset in range(1, models)]
            codes = call(code_kernel, jax.ShapeDtypeStruct((3, span, width), jnp.int16))(
                over_y, over_z, far, after=x_near + ([] if k else other_weights)
            )
            all_codes = [outs[0], codes]
            for offset in range(1, models):
                all_codes += [x_near[offset - 1], rotate(codes, "mp", offset)]
    early = call(
        functools.partial(early_merge_kernel, models, tile_width, starts[-1], widths[-1], code_scale),
        jax.ShapeDtypeStruct((4, span, widths[-1]), jnp.float32),
    )(weights, *other_weights, *all_codes, after=nears)
    operands = [early, *nears, weights, *other_weights, *chunks]
    result = pl.pallas_call(
        functools.partial(last_merge_kernel, models, tile_width, starts, widths, code_scale),
        out_shape=jax.ShapeDtypeStruct(weights.shape, jnp.float32),
        in_specs=[VMEM] * len(operands),
        out_specs=pl.BlockSpec(memory_space=pltpu.HBM),
        scratch_shapes=[
            pltpu.VMEM((2, span, tile_width), jnp.float32),
            pltpu.SemaphoreType.DMA((4 * len(widths),)),
        ],
        compiler_params=pltpu.CompilerParams(vmem_limit_bytes=VMEM_LIMIT),
    )(*operands)
    return result[None]


def solution(mesh):
    models, devices = mesh.shape["mp"], mesh.shape["tok"]
    grid = Mesh(mesh.devices.reshape(models, 2, 2, ROW_BLOCKS // 4, devices // ROW_BLOCKS), ("mp",) + TOK)
    in_specs = (
        P("mp", TOK, None, None),
        P("mp", TOK, None, None),
        P("mp", TOK, None),
        P("mp", TOK, None, None),
    )
    return jax.shard_map(shards, mesh=grid, in_specs=in_specs, out_specs=P(TOK, None, None), check_vma=False)
```
